128 devices in a mesh: ctx: 32 (over z, y, core), tp: 4 (over x).
Axes of the slice: x: 4, y: 4, z: 4, core: 2. Of those that a mesh axis runs over, the one named last changes fastest.
Arguments:
- x_tokens: bfloat16 [16384, 4096], P('ctx', 'tp'), may hold values from -60 to 60
- w_query: bfloat16 [4096, 4096], P(None, 'tp'), may hold values from -0.09375 to 0.09375
- w_key: bfloat16 [4096, 1024], P(None, 'tp'), may hold values from -0.09375 to 0.09375
- w_value: bfloat16 [4096, 1024], P(None, 'tp'), may hold values from -0.09375 to 0.09375
- w_output: bfloat16 [4096, 4096], P('tp'), may hold values from -0.09375 to 0.09375
- pattern: int32 [128, 8], P('ctx'), may hold values from 0 to 127, as said below
- doc_lengths: int32 [16], replicated, may hold values from 1 to 10240, 16384 in all
Outputs:
- attn_out: bfloat16 [16384, 4096], P(('ctx', 'tp'))
The draws below stay inside these ranges and needn't reach their ends.
Inputs may be any that keep to these rules, and one draw needn't show every extreme that they name: `pattern`: row q has 8 entries; the first is q itself and every entry is at most q; entries may repeat. The rows of one index of ctx (4 rows) name at most 2 distinct blocks held by any other index of ctx (index i holding blocks i * 4 onward), and exactly 2 of index 0 for every other index. Every row of an index i in the upper half of ctx names 2 blocks of index i minus half the number of ctx indices.
All inputs are finite; a program needn't handle non-finite values.
Results may differ from the reference program's by a relative error of at most 0.02.
Values may be sent and summed in bfloat16 or wider, within the bound.
No kernel may reach another device: no remote copies, remote signals or barrier semaphores. Data moves between devices by JAX's collectives and lax.ppermute only.
A program may use at most 128 MiB of HBM per device.

```python
import math
import jax
import jax.numpy as jnp
import numpy as np
from jax import lax

D = 4096
HQ = 32
KV = 8
HD = 128
BLK = 128
LIST = 8
CAP = 2
TOK_DEV = 512
TOKENS = 16384
NQB = 128
NDOCS = 16
MOST = 10240


def draw_x_tokens(key, part):
    first_key = jax.random.fold_in(key, 0)
    return jnp.clip(jax.random.normal(first_key, (TOKENS, D), jnp.float32), -6.0, 6.0).astype(jnp.bfloat16)


def draw_pattern(key, part):
    first_key, second_key, third_key, fourth_key, fifth_key = jax.random.split(key, 5)
    per_device = TOK_DEV // BLK
    device_count = NQB // per_device
    half_count = device_count // 2
    block_ids = jnp.arange(NQB, dtype=jnp.int32)[:, None]
    owner_ids = block_ids // per_device
    shape_rest = (NQB, LIST - 1)
    near_source = jnp.maximum(owner_ids - jax.random.randint(first_key, shape_rest, 0, 4), 0)
    wide_source = jax.random.randint(second_key, shape_rest, 0, jnp.broadcast_to(owner_ids + 1, shape_rest))
    picker = jax.random.randint(third_key, shape_rest, 0, 2)
    source = jnp.where(picker == 1, near_source, wide_source)
    slot_pick = jax.random.randint(fourth_key, shape_rest, 0, CAP)
    column = jnp.arange(LIST - 1, dtype=jnp.int32)[None, :]
    far_forced = (owner_ids >= half_count) & (column >= CAP) & (column < 2 * CAP)
    source = jnp.where(far_forced, owner_ids - half_count, source)
    slot_pick = jnp.where(far_forced, column - CAP, slot_pick)
    forced = (block_ids % per_device == 0) & (owner_ids >= 1) & (column < CAP)
    source = jnp.where(forced, 0, source)
    slot_pick = jnp.where(forced, column, slot_pick)
    offset_table = jax.random.randint(fifth_key, (device_count, device_count), 0, per_device)
    offset_here = offset_table[jnp.broadcast_to(owner_ids, shape_rest), source]
    chosen = source * per_device + (offset_here + slot_pick) % per_device
    chosen = jnp.minimum(chosen, block_ids)
    return jnp.concatenate([block_ids, chosen], axis=1).astype(jnp.int32)


def steps_of(own_key, extent, shards, smallest, top_value):
    loudness = 1.0
    for axis_at, shards_of in shards:
        heights = jax.random.uniform(jax.random.fold_in(jax.random.fold_in(own_key, 6), axis_at), (shards_of,), jnp.float32, smallest / len(shards), top_value / len(shards))
        loudness = loudness * jnp.repeat(jnp.exp(heights), extent[axis_at] // shards_of).reshape((-1,) + (1,) * (len(extent) - 1 - axis_at))
    return loudness


def profile(count, total, bound, skew):
    weights = [(1 << 20) // math.isqrt(grade ** skew) + 1 for grade in range(2, count + 1)]
    spare, counts = total - bound - (count - 1), [1] * (count - 1)
    while spare > 0:
        free = [i for i in range(count - 1) if counts[i] < bound]
        pool, budget = sum([weights[i] for i in free]), spare
        for i in free:
            extra = min(bound - counts[i], max(1, budget * weights[i] // pool), spare)
            counts[i] = counts[i] + extra
            spare = spare - extra
    return np.array([bound] + counts)


def uneven(key, count, total, bound, lean):
    if count == 2:
        one = jax.random.randint(key, (), max(1, total - bound), min(bound, total - 1) + 1)
        return jnp.stack([one, total - one])
    lengths = jnp.asarray(profile(count, total, bound, lean), jnp.int32)
    pairs = (count - 1) // 2
    giver, sink = lengths[1:1 + 2 * pairs:2], lengths[2:2 + 2 * pairs:2]
    slack = jnp.minimum(giver - 1, bound - sink)
    passed = jax.random.randint(jax.random.fold_in(key, 1), (pairs,), 0, 1 << 20) % (slack + 1)
    lengths = lengths.at[1:1 + 2 * pairs:2].set(giver - passed).at[2:2 + 2 * pairs:2].set(sink + passed)
    return lengths[jax.random.permutation(jax.random.fold_in(key, 2), count)]


def scatter_about(stream_key, dims, deviation, reach, pieces=(), kind=jnp.bfloat16):
    gain = steps_of(stream_key, dims, pieces, -0.22, 0.18) if pieces else 1.0
    values = jax.random.normal(stream_key, dims, jnp.float32) * deviation * gain
    return jnp.minimum(jnp.maximum(values, -reach), reach).astype(kind)


def setup_inputs(seed: int = 0) -> dict:
    key_of = jax.random.split(jax.random.key(seed), 8)
    return {
        "x_tokens": draw_x_tokens(jax.random.fold_in(key_of[7], 71), 0),
        "w_query": scatter_about(key_of[1], (D, HQ * HD), D ** -0.5, 0.09375, ((1, 4),)),
        "w_key": scatter_about(key_of[2], (D, KV * HD), D ** -0.5, 0.09375, ((1, 4),)),
        "w_value": scatter_about(key_of[3], (D, KV * HD), D ** -0.5, 0.09375, ((1, 4),)),
        "w_output": scatter_about(key_of[4], (HQ * HD, D), (HQ * HD) ** -0.5, 0.09375, ((0, 4),)),
        "pattern": draw_pattern(jax.random.fold_in(key_of[7], 71), 0),
        "doc_lengths": uneven(key_of[6], NDOCS, TOKENS, MOST, 2).astype(jnp.int32),
    }


ROPE_BASE = 500000.0
NEG_LARGE = -1e30


def rotate(projected, head_count, positions):
    split_heads = projected.reshape(projected.shape[0], head_count, HD)
    frequency = ROPE_BASE ** (-(jnp.arange(HD // 2, dtype=jnp.float32) * 2.0 / HD))
    angles = positions.astype(jnp.float32)[:, None] * frequency[None, :]
    cosine_table = jnp.cos(angles)[:, None, :]
    sine_table = jnp.sin(angles)[:, None, :]
    front_half = split_heads[..., : HD // 2]
    back_half = split_heads[..., HD // 2:]
    return jnp.concatenate([front_half * cosine_table - back_half * sine_table, back_half * cosine_table + front_half * sine_table], axis=-1)


def document_of(positions, doc_lengths):
    ends = jnp.cumsum(doc_lengths).astype(jnp.int32)
    return jnp.sum((ends[None, :] <= positions[:, None]).astype(jnp.int32), axis=1)


def fresh_entries(pattern):
    equal = pattern[:, :, None] == pattern[:, None, :]
    earlier = jnp.tril(jnp.ones((LIST, LIST), dtype=bool), -1)
    return jnp.logical_not(jnp.any(equal & earlier[None], axis=2))


def reference(x_tokens, w_query, w_key, w_value, w_output, pattern, doc_lengths):
    positions = jnp.arange(TOKENS, dtype=jnp.int32)
    group_size = HQ // KV
    query = rotate(jnp.dot(x_tokens, w_query, preferred_element_type=jnp.float32), HQ, positions) * (HD ** -0.5)
    query = lax.optimization_barrier(query.astype(jnp.bfloat16)).astype(jnp.float32).reshape(TOKENS, KV, group_size, HD)
    keys = rotate(jnp.dot(x_tokens, w_key, preferred_element_type=jnp.float32), KV, positions)
    keys = lax.optimization_barrier(keys.astype(jnp.bfloat16)).astype(jnp.float32)
    values = jnp.dot(x_tokens, w_value, preferred_element_type=jnp.float32)
    values = lax.optimization_barrier(values.astype(jnp.bfloat16)).astype(jnp.float32).reshape(TOKENS, KV, HD)
    documents = document_of(positions, doc_lengths)
    fresh = fresh_entries(pattern)
    offsets_in = jnp.arange(BLK, dtype=jnp.int32)

    def one_block(block):
        listed = pattern[block]
        keep = fresh[block]
        key_index = (listed[:, None] * BLK + offsets_in[None, :]).reshape(-1).astype(jnp.int32)
        key_ok = jnp.repeat(keep, BLK)
        row_index = (block * BLK + offsets_in).astype(jnp.int32)
        rows_query = lax.dynamic_slice_in_dim(query, (block * BLK).astype(jnp.int32), BLK, 0)
        scores = jnp.einsum("qkgd,lkd->kgql", rows_query, keys[key_index])
        allowed = (key_index[None, :] <= row_index[:, None]) & (documents[key_index][None, :] == documents[row_index][:, None]) & key_ok[None, :]
        masked = jnp.where(allowed, scores, NEG_LARGE)
        row_max = jnp.max(masked, axis=-1, keepdims=True)
        weights = jnp.where(allowed, jnp.exp(masked - row_max), 0.0)
        total = jnp.sum(weights, axis=-1)
        rounded = lax.optimization_barrier(weights.astype(jnp.bfloat16)).astype(jnp.float32)
        mixed = jnp.einsum("kgql,lkd->kgqd", rounded, values[key_index]) / total[..., None]
        return jnp.transpose(mixed, (2, 0, 1, 3)).reshape(BLK, HQ * HD).astype(jnp.bfloat16)

    attended = lax.map(one_block, jnp.arange(NQB, dtype=jnp.int32)).reshape(TOKENS, HQ * HD)
    return jnp.dot(attended, w_output, preferred_element_type=jnp.float32).astype(jnp.bfloat16)
```

```python
import functools

import jax
import jax.numpy as jnp
from jax import lax
from jax.experimental import pallas as pl
from jax.experimental.pallas import tpu as pltpu
from jax.sharding import PartitionSpec as P

HD = 128
BLK = 128
LIST = 8
ROPE_BASE = 500000.0
NEG_LARGE = -1e30
CHUNKS = 2
VMEM = 20 << 20
BF16 = jnp.bfloat16
F32 = jnp.float32


def ctx_index(z, y, c):
    return ((z % 4) * 4 + (y % 4)) * 2 + c


def plane_pairs(step, first):
    pairs = []
    for z in range(4):
        for y in range(4):
            for c in range(2):
                along_z = (c == 0) == first
                to = ctx_index(z + step, y, c) if along_z else ctx_index(z, y + step, c)
                pairs.append((ctx_index(z, y, c), to))
    return pairs


CORE_PAIRS = [(i, i ^ 1) for i in range(32)]


def tp_pairs(step):
    return [(i, (i + step) % 4) for i in range(4)]


def core_swap(u):
    return lax.ppermute(u, "ctx", CORE_PAIRS)


def send_tp(u, step):
    return lax.ppermute(u, "tp", tp_pairs(step))


def send_one(u, step):
    return lax.ppermute(u, "ctx", plane_pairs(step, True))


def send_two(u, step):
    return lax.ppermute(u, "ctx", plane_pairs(step, False))


def roped(u, cosine, sine):
    return u * cosine + pltpu.roll(u, HD // 2, 1) * sine


def kv_kernel(ids, own, before, after, far, wk, wv, cos, sin, mine, theirs, tk, tv):
    step = pl.program_id(0)
    for at, ref in enumerate((own, before, after, far)):

        @pl.when(step == at)
        def _(at=at, ref=ref):
            for w, total in ((wk, tk), (wv, tv)):
                part = jnp.dot(ref[...], w[...], preferred_element_type=F32)
                if at == 0:
                    total[...] = part
                else:
                    total[...] += part

    @pl.when(step == 3)
    def _():
        cosine, sine = cos[...], sin[...]
        heads = [roped(tk[:, h * HD : (h + 1) * HD], cosine, sine).astype(BF16) for h in range(2)]
        vals = [tv[:, h * HD : (h + 1) * HD].astype(BF16) for h in range(2)]

        for core in range(2):

            @pl.when(ids[4] == core)
            def _(core=core):
                mine[:, :HD] = heads[core]
                mine[:, HD:] = vals[core]
                theirs[:, :HD] = heads[1 - core]
                theirs[:, HD:] = vals[1 - core]


def project_kv(ids, sources, wk, wv, cos, sin):
    rows, depth = sources[0].shape
    whole = lambda u: pl.BlockSpec(u.shape, lambda k, ids: (0, 0))
    w_spec = pl.BlockSpec((depth, 2 * HD), lambda k, ids: (ids[k], 0))
    out = jax.ShapeDtypeStruct((rows, 2 * HD), BF16)
    return pl.pallas_call(
        kv_kernel,
        grid_spec=pltpu.PrefetchScalarGridSpec(
            num_scalar_prefetch=1,
            grid=(4,),
            in_specs=[whole(u) for u in sources] + [w_spec, w_spec, whole(cos), whole(sin)],
            out_specs=[pl.BlockSpec((rows, 2 * HD), lambda k, ids: (0, 0))] * 2,
            scratch_shapes=[pltpu.VMEM((rows, 2 * HD), F32)] * 2,
        ),
        out_shape=[out, out],
        compiler_params=pltpu.CompilerParams(vmem_limit_bytes=VMEM),
        cost_estimate=pl.CostEstimate(
            flops=2 * rows * 4 * depth * 4 * HD, bytes_accessed=6 << 20, transcendentals=0
        ),
    )(ids, *sources, wk, wv, cos, sin)


def q_kernel(ids, *refs):
    parts, (wq, cos, sin, out) = [refs[4 * k : 4 * k + 4] for k in range(CHUNKS)], refs[4 * CHUNKS :]
    depth = parts[0][0].shape[1]
    at = [pl.ds(pl.multiple_of(ids[k] * depth, depth), depth) for k in range(4)]
    for chunk, sources in enumerate(parts):
        rows = sources[0].shape[0]
        span = slice(chunk * rows, (chunk + 1) * rows)
        total = sum(jnp.dot(sources[k][...], wq[at[k], :], preferred_element_type=F32) for k in range(4))
        cosine, sine = cos[span, :], sin[span, :]
        for h in range(2):
            turned = roped(total[:, h * HD : (h + 1) * HD], cosine, sine) * HD ** (-0.5)
            out[span, h * HD : (h + 1) * HD] = turned.astype(BF16)


def project_q(ids, side, sources, wq, cos, sin):
    rows, inner = cos.shape[0], wq.shape[0]
    flat = [u for part in sources for u in part]
    whole = lambda u: pl.BlockSpec(u.shape, lambda j, ids: (0, 0))
    return pl.pallas_call(
        q_kernel,
        grid_spec=pltpu.PrefetchScalarGridSpec(
            num_scalar_prefetch=1,
            grid=(2,),
            in_specs=[whole(u) for u in flat]
            + [
                pl.BlockSpec((inner, 2 * HD), lambda j, ids: (0, 2 * ids[4 + side] + j)),
                whole(cos),
                whole(sin),
            ],
            out_specs=pl.BlockSpec((rows, 2 * HD), lambda j, ids: (0, j)),
        ),
        out_shape=jax.ShapeDtypeStruct((rows, 4 * HD), BF16),
        compiler_params=pltpu.CompilerParams(vmem_limit_bytes=VMEM),
        cost_estimate=pl.CostEstimate(
            flops=2 * rows * inner * 4 * HD, bytes_accessed=8 << 20, transcendentals=0
        ),
    )(ids, *flat, wq, cos, sin)


def pack_kernel(*refs):
    parts, out = refs[:-1], refs[-1]
    rows = parts[0].shape[0]
    for k, u in enumerate(parts):
        out[k * rows : (k + 1) * rows, :] = u[...]


def pack(*parts):
    rows, cols = parts[0].shape
    vmem = pl.BlockSpec(memory_space=pltpu.VMEM)
    return pl.pallas_call(
        pack_kernel,
        in_specs=[vmem] * len(parts),
        out_specs=vmem,
        out_shape=jax.ShapeDtypeStruct((len(parts) * rows, cols), parts[0].dtype),
        compiler_params=pltpu.CompilerParams(vmem_limit_bytes=VMEM),
        cost_estimate=pl.CostEstimate(flops=0, bytes_accessed=2 * len(parts) * rows * cols * 2, transcendentals=0),
    )(*parts)


def attend_kernel(side, offsets, n_arrays, ids, table, lengths, query, *rest):
    arrays, (out, held, arrived) = rest[:n_arrays], rest[n_arrays:]
    count = len(offsets)
    blocks = [lax.rem(ids[0] + off, 4) for off in offsets]

    for n, block in enumerate(blocks):

        def fetch(e, carry, n=n, block=block):
            entry = n * LIST + e
            place = table[(side * 4 + block) * LIST + e]

            def from_array(ref):
                def go():
                    row = pl.multiple_of(lax.rem(place, 64) * BLK, BLK)
                    pltpu.make_async_copy(
                        ref.at[pl.ds(row, BLK), :],
                        held.at[pl.ds(pl.multiple_of(entry * BLK, BLK), BLK), :],
                        arrived.at[entry],
                    ).start()

                return go

            lax.switch(lax.div(place, 64), [from_array(r) for r in arrays])
            return carry

        lax.fori_loop(0, LIST, fetch, 0)

    rows = lax.broadcasted_iota(jnp.int32, (BLK, BLK), 0)
    lanes = lax.broadcasted_iota(jnp.int32, (BLK, BLK), 1)
    for n, block in enumerate(blocks):
        at = pl.ds(pl.multiple_of(block * BLK, BLK), BLK)
        position = rows + (ids[6 + side] + block * BLK)
        begin, end = jnp.zeros_like(rows), 0
        for d in range(lengths.shape[0]):
            end = end + lengths[d]
            begin = jnp.where(position >= end, end, begin)
        bias = []
        for e in range(LIST):
            index = lanes + table[(8 + side * 4 + block) * LIST + e]
            bias.append(jnp.where((index <= position) & (index >= begin), 0.0, NEG_LARGE))
        bias = jnp.concatenate(bias, axis=1)
        for e in range(LIST):
            entry = n * LIST + e
            pltpu.make_async_copy(
                arrays[0].at[pl.ds(0, BLK), :], held.at[pl.ds(entry * BLK, BLK), :], arrived.at[entry]
            ).wait()
        span = slice(n * LIST * BLK, (n + 1) * LIST * BLK)
        keys = held[span, :HD]
        values = held[span, HD:]
        part = jnp.concatenate([query[at, h * HD : (h + 1) * HD] for h in range(4)])
        scores = lax.dot_general(part, keys, (((1,), (1,)), ((), ())), preferred_element_type=F32)
        rounded, totals = [], []
        for h in range(4):
            masked = scores[h * BLK : (h + 1) * BLK] + bias
            weights = jnp.exp(masked - jnp.max(masked, axis=1, keepdims=True))
            totals.append(jnp.sum(weights, axis=1, keepdims=True))
            rounded.append(weights.astype(BF16))
        mixed = jnp.dot(jnp.concatenate(rounded), values, preferred_element_type=F32)
        for h in range(4):
            done = mixed[h * BLK : (h + 1) * BLK] / totals[h]
            out[n * BLK : (n + 1) * BLK, h * HD : (h + 1) * HD] = done.astype(BF16)


def attend(side, offsets, ids, table, lengths, query, arrays):
    count = len(offsets)
    smem = pl.BlockSpec(memory_space=pltpu.SMEM)
    vmem = pl.BlockSpec(memory_space=pltpu.VMEM)
    work = count * 4 * BLK * LIST * BLK
    return pl.pallas_call(
        functools.partial(attend_kernel, side, offsets, len(arrays)),
        in_specs=[smem] * 3 + [vmem] + [pl.BlockSpec(memory_space=pl.ANY)] * len(arrays),
        out_specs=vmem,
        out_shape=jax.ShapeDtypeStruct((count * BLK, 4 * HD), BF16),
        scratch_shapes=[
            pltpu.VMEM((count * LIST * BLK, 2 * HD), BF16),
            pltpu.SemaphoreType.DMA((count * LIST,)),
        ],
        compiler_params=pltpu.CompilerParams(vmem_limit_bytes=VMEM),
        cost_estimate=pl.CostEstimate(
            flops=4 * work * HD, bytes_accessed=count << 20, transcendentals=work
        ),
    )(ids, table, lengths, query, *arrays)


def heads_in_order(core, mine, other):
    return jnp.concatenate(
        [jnp.where(core == 0, mine, other), jnp.where(core == 0, other, mine)], axis=1
    )


def far_kernel(core, mine, other, w_left, w_right, left, right):
    rows = heads_in_order(core[0], mine[...], other[...])
    left[...] = jnp.dot(rows, w_left[...], preferred_element_type=F32).astype(BF16)
    right[...] = jnp.dot(rows, w_right[...], preferred_element_type=F32).astype(BF16)


TILE = 512


def project_far(core, mine, other, wo):
    rows, cols = mine.shape[0], wo.shape[1]
    n = cols // TILE // 2
    whole = pl.BlockSpec(mine.shape, lambda j, core: (0, 0))
    out = jax.ShapeDtypeStruct((rows, cols // 2), BF16)
    return pl.pallas_call(
        far_kernel,
        grid_spec=pltpu.PrefetchScalarGridSpec(
            num_scalar_prefetch=1,
            grid=(n,),
            in_specs=[
                whole,
                whole,
                pl.BlockSpec((wo.shape[0], TILE), lambda j, core: (0, j)),
                pl.BlockSpec((wo.shape[0], TILE), lambda j, core: (0, j + n)),
            ],
            out_specs=[pl.BlockSpec((rows, TILE), lambda j, core: (0, j))] * 2,
        ),
        out_shape=[out, out],
        compiler_params=pltpu.CompilerParams(vmem_limit_bytes=VMEM),
        cost_estimate=pl.CostEstimate(
            flops=2 * rows * wo.shape[0] * cols, bytes_accessed=10 << 20, transcendentals=0
        ),
    )(core, mine, other, wo, wo)


def near_kernel(n, core, mine, other, w, left, right, to_after, to_before):
    j = pl.program_id(0)
    rows = heads_in_order(core[0], mine[...], other[...])
    part = jnp.dot(rows, w[...], preferred_element_type=F32)

    @pl.when(j < n)
    def _():
        to_after[...] = (part[:BLK] + left[...].astype(F32)).astype(BF16)
        to_before[...] = part[BLK:].astype(BF16)

    @pl.when(j >= n)
    def _():
        to_after[...] = part[:BLK].astype(BF16)
        to_before[...] = (part[BLK:] + right[...].astype(F32)).astype(BF16)


def project_near(core, mine, other, wo, left, right):
    cols = wo.shape[1]
    n = cols // TILE // 2
    whole = pl.BlockSpec(mine.shape, lambda j, core: (0, 0))
    out = jax.ShapeDtypeStruct((BLK, cols), BF16)
    return pl.pallas_call(
        functools.partial(near_kernel, n),
        grid_spec=pltpu.PrefetchScalarGridSpec(
            num_scalar_prefetch=1,
            grid=(2 * n,),
            in_specs=[
                whole,
                whole,
                pl.BlockSpec((wo.shape[0], TILE), lambda j, core: (0, j)),
                pl.BlockSpec((BLK, TILE), lambda j, core: (0, jnp.minimum(j, n - 1))),
                pl.BlockSpec((BLK, TILE), lambda j, core: (0, jnp.maximum(j - n, 0))),
            ],
            out_specs=[pl.BlockSpec((BLK, TILE), lambda j, core: (0, j))] * 2,
        ),
        out_shape=[out, out],
        compiler_params=pltpu.CompilerParams(vmem_limit_bytes=VMEM),
        cost_estimate=pl.CostEstimate(
            flops=4 * BLK * wo.shape[0] * cols, bytes_accessed=11 << 20, transcendentals=0
        ),
    )(core, mine, other, wo, left, right)


def own_kernel(core, mine, other, w, out):
    rows = heads_in_order(core[0], mine[...], other[...])
    out[...] = jnp.dot(rows, w[...], preferred_element_type=F32)


def project_own(core, mine, other, wo):
    cols = wo.shape[1]
    whole = pl.BlockSpec(mine.shape, lambda j, core: (0, 0))
    return pl.pallas_call(
        own_kernel,
        grid_spec=pltpu.PrefetchScalarGridSpec(
            num_scalar_prefetch=1,
            grid=(cols // TILE,),
            in_specs=[whole, whole, pl.BlockSpec((wo.shape[0], TILE), lambda j, core: (0, j))],
            out_specs=pl.BlockSpec((BLK, TILE), lambda j, core: (0, j)),
        ),
        out_shape=jax.ShapeDtypeStruct((BLK, cols), F32),
        compiler_params=pltpu.CompilerParams(vmem_limit_bytes=VMEM),
        cost_estimate=pl.CostEstimate(
            flops=2 * BLK * wo.shape[0] * cols, bytes_accessed=10 << 20, transcendentals=0
        ),
    )(core, mine, other, wo)


def rope_tables(positions):
    frequency = ROPE_BASE ** (-(jnp.arange(HD // 2, dtype=F32) * 2.0 / HD))
    angles = positions.astype(F32)[:, None] * frequency[None, :]
    cosine, sine = jnp.cos(angles), jnp.sin(angles)
    return jnp.concatenate([cosine, cosine], axis=1), jnp.concatenate([-sine, sine], axis=1)


def fresh_entries(pattern):
    equal = pattern[:, :, None] == pattern[:, None, :]
    earlier = jnp.tril(jnp.ones((LIST, LIST), dtype=bool), -1)
    return jnp.logical_not(jnp.any(equal & earlier[None], axis=2))


def block_places(pattern, me):
    core, y, z = me % 2, (me // 2) % 4, me // 8
    per = 4 // CHUNKS
    chip = pattern // 8
    from_z, from_y = chip // 4, chip % 4
    other, local = ((pattern // 4) % 2 != core).astype(jnp.int32), pattern % 4
    along_one = jnp.where(core == 0, z - from_z, y - from_y) % 4
    along_two = jnp.where(core == 0, y - from_y, z - from_z) % 4
    slots = [jnp.where(u == 3, 2, jnp.where(u == 2, 3, u)) for u in (along_one, along_two)]
    array = (local // per) * 8 + slots[1] * 2 + other
    return array * 64 + slots[0] * per + local % per


def after(u, *others):
    return lax.optimization_barrier((u, *others))[0]


def on_device(x_tokens, w_query, w_key, w_value, w_output, pattern, doc_lengths):
    rows = x_tokens.shape[0]
    tp, me = lax.axis_index("tp"), lax.axis_index("ctx")
    core = me % 2
    length = rows // CHUNKS
    ids = jnp.stack(
        [tp, (tp + 3) % 4, (tp + 1) % 4, (tp + 2) % 4, core, 1 - core, me * rows, (me ^ 1) * rows]
    ).astype(jnp.int32)
    cos, sin = rope_tables(me * rows + jnp.arange(rows, dtype=jnp.int32))
    listed = jnp.concatenate([pattern, core_swap(pattern)])
    base = jnp.where(fresh_entries(listed), listed * BLK, 1 << 24)
    table = jnp.concatenate([block_places(listed, me), base]).astype(jnp.int32).reshape(-1)

    first, second = x_tokens[:length], x_tokens[length:]
    first_before, first_after = send_tp(first, 1), send_tp(first, -1)
    first_far = send_tp(after(first_before, ids, cos, sin, table), 1)
    second_after = send_tp(after(second, first_after), -1)
    second_before = send_tp(after(second, first_far), 1)
    second_far = send_tp(second_after, -1)
    sources = [
        (first, first_before, first_after, first_far),
        (second, second_before, second_after, second_far),
    ]

    gathered, query = [], []
    for chunk in range(CHUNKS):
        part = slice(chunk * length, (chunk + 1) * length)
        mine, theirs = project_kv(ids, sources[chunk], w_key, w_value, cos[part], sin[part])
        other = core_swap(theirs)
        lines = []
        for u, way in ((mine, 1), (other, -1)):
            near = {step: send_one(u, step) for step in (1, -1)}
            lines.append(pack(u, near[1], near[-1], send_one(near[way], way)))
        nears = [{step: send_two(u, step) for step in (1, -1)} for u in lines]
        made = project_q(ids, 1 - chunk, sources, w_query, cos, sin)
        query.append(made if chunk else core_swap(made))
        fars = [send_two(after(near[way], made), way) for near, way in zip(nears, (1, -1))]
        gathered += [*lines, *[near[1] for near in nears], *[near[-1] for near in nears], *fars]

    def attended(*offsets):
        other = core_swap(attend(1, offsets, ids, table, doc_lengths, query[0], gathered))
        return attend(0, offsets, ids, table, doc_lengths, query[1], gathered), other

    core_id = ids[4:5]
    left, right = project_far(core_id, *attended(2), w_output)
    left, right = send_tp(left, 1), send_tp(right, -1)
    to_after, to_before = project_near(core_id, *attended(1, 3), w_output, left, right)
    from_before, from_after = send_tp(to_after, 1), send_tp(to_before, -1)
    own = project_own(core_id, *attended(0), w_output)
    return (own + from_before.astype(F32) + from_after.astype(F32)).astype(BF16)


def solution(mesh):
    return jax.shard_map(
        on_device,
        mesh=mesh,
        in_specs=(
            P("ctx", "tp"),
            P(None, "tp"),
            P(None, "tp"),
            P(None, "tp"),
            P("tp", None),
            P("ctx", None),
            P(),
        ),
        out_specs=P(("ctx", "tp"), None),
        check_vma=False,
    )
```

```python
import functools

import jax
import jax.numpy as jnp
from jax import lax
from jax.experimental import pallas as pl
from jax.experimental.pallas import tpu as pltpu
from jax.sharding import PartitionSpec as P

HD = 128
BLK = 128
LIST = 8
ROPE_BASE = 500000.0
NEG_LARGE = -1e30
CHUNKS = 2
VMEM = 20 << 20
BF16 = jnp.bfloat16
F32 = jnp.float32


def ctx_index(z, y, c):
    return ((z % 4) * 4 + (y % 4)) * 2 + c


def plane_pairs(step, first):
    pairs = []
    for z in range(4):
        for y in range(4):
            for c in range(2):
                along_z = (c == 0) == first
                to = ctx_index(z + step, y, c) if along_z else ctx_index(z, y + step, c)
                pairs.append((ctx_index(z, y, c), to))
    return pairs


CORE_PAIRS = [(i, i ^ 1) for i in range(32)]


def tp_pairs(step):
    return [(i, (i + step) % 4) for i in range(4)]


def core_swap(u):
    return lax.ppermute(u, "ctx", CORE_PAIRS)


def send_tp(u, step):
    return lax.ppermute(u, "tp", tp_pairs(step))


def send_one(u, step):
    return lax.ppermute(u, "ctx", plane_pairs(step, True))


def send_two(u, step):
    return lax.ppermute(u, "ctx", plane_pairs(step, False))


def roped(u, cosine, sine):
    return u * cosine + pltpu.roll(u, HD // 2, 1) * sine


def kv_kernel(ids, own, before, after, far, wk, wv, cos, sin, mine, theirs, tk, tv):
    step = pl.program_id(0)
    for at, ref in enumerate((own, before, after, far)):

        @pl.when(step == at)
        def _(at=at, ref=ref):
            for w, total in ((wk, tk), (wv, tv)):
                part = jnp.dot(ref[...], w[...], preferred_element_type=F32)
                if at == 0:
                    total[...] = part
                else:
                    total[...] += part

    @pl.when(step == 3)
    def _():
        cosine, sine = cos[...], sin[...]
        heads = [roped(tk[:, h * HD : (h + 1) * HD], cosine, sine).astype(BF16) for h in range(2)]
        vals = [tv[:, h * HD : (h + 1) * HD].astype(BF16) for h in range(2)]

        for core in range(2):

            @pl.when(ids[4] == core)
            def _(core=core):
                mine[:, :HD] = heads[core]
                mine[:, HD:] = vals[core]
                theirs[:, :HD] = heads[1 - core]
                theirs[:, HD:] = vals[1 - core]


def project_kv(ids, sources, wk, wv, cos, sin):
    rows, depth = sources[0].shape
    whole = lambda u: pl.BlockSpec(u.shape, lambda k, ids: (0, 0))
    w_spec = pl.BlockSpec((depth, 2 * HD), lambda k, ids: (ids[k], 0))
    out = jax.ShapeDtypeStruct((rows, 2 * HD), BF16)
    return pl.pallas_call(
        kv_kernel,
        grid_spec=pltpu.PrefetchScalarGridSpec(
            num_scalar_prefetch=1,
            grid=(4,),
            in_specs=[whole(u) for u in sources] + [w_spec, w_spec, whole(cos), whole(sin)],
            out_specs=[pl.BlockSpec((rows, 2 * HD), lambda k, ids: (0, 0))] * 2,
            scratch_shapes=[pltpu.VMEM((rows, 2 * HD), F32)] * 2,
        ),
        out_shape=[out, out],
        compiler_params=pltpu.CompilerParams(vmem_limit_bytes=VMEM),
        cost_estimate=pl.CostEstimate(
            flops=2 * rows * 4 * depth * 4 * HD, bytes_accessed=6 << 20, transcendentals=0
        ),
    )(ids, *sources, wk, wv, cos, sin)


def q_kernel(ids, *refs):
    parts, (wq, cos, sin, out) = [refs[4 * k : 4 * k + 4] for k in range(CHUNKS)], refs[4 * CHUNKS :]
    depth = parts[0][0].shape[1]
    at = [pl.ds(pl.multiple_of(ids[k] * depth, depth), depth) for k in range(4)]
    for chunk, sources in enumerate(parts):
        rows = sources[0].shape[0]
        span = slice(chunk * rows, (chunk + 1) * rows)
        total = sum(jnp.dot(sources[k][...], wq[at[k], :], preferred_element_type=F32) for k in range(4))
        cosine, sine = cos[span, :], sin[span, :]
        for h in range(2):
            turned = roped(total[:, h * HD : (h + 1) * HD], cosine, sine) * HD ** (-0.5)
            out[span, h * HD : (h + 1) * HD] = turned.astype(BF16)


def project_q(ids, side, sources, wq, cos, sin):
    rows, inner = cos.shape[0], wq.shape[0]
    flat = [u for part in sources for u in part]
    whole = lambda u: pl.BlockSpec(u.shape, lambda j, ids: (0, 0))
    return pl.pallas_call(
        q_kernel,
        grid_spec=pltpu.PrefetchScalarGridSpec(
            num_scalar_prefetch=1,
            grid=(2,),
            in_specs=[whole(u) for u in flat]
            + [
                pl.BlockSpec((inner, 2 * HD), lambda j, ids: (0, 2 * ids[4 + side] + j)),
                whole(cos),
                whole(sin),
            ],
            out_specs=pl.BlockSpec((rows, 2 * HD), lambda j, ids: (0, j)),
        ),
        out_shape=jax.ShapeDtypeStruct((rows, 4 * HD), BF16),
        compiler_params=pltpu.CompilerParams(vmem_limit_bytes=VMEM),
        cost_estimate=pl.CostEstimate(
            flops=2 * rows * inner * 4 * HD, bytes_accessed=8 << 20, transcendentals=0
        ),
    )(ids, *flat, wq, cos, sin)


def pack_kernel(*refs):
    parts, out = refs[:-1], refs[-1]
    rows = parts[0].shape[0]
    for k, u in enumerate(parts):
        out[k * rows : (k + 1) * rows, :] = u[...]


def pack(*parts):
    rows, cols = parts[0].shape
    vmem = pl.BlockSpec(memory_space=pltpu.VMEM)
    return pl.pallas_call(
        pack_kernel,
        in_specs=[vmem] * len(parts),
        out_specs=vmem,
        out_shape=jax.ShapeDtypeStruct((len(parts) * rows, cols), parts[0].dtype),
        compiler_params=pltpu.CompilerParams(vmem_limit_bytes=VMEM),
        cost_estimate=pl.CostEstimate(flops=0, bytes_accessed=2 * len(parts) * rows * cols * 2, transcendentals=0),
    )(*parts)


def attend_kernel(side, offsets, n_arrays, ids, table, lengths, query, *rest):
    arrays, (out, held) = rest[:n_arrays], rest[n_arrays:]
    count = len(offsets)
    blocks = [lax.rem(ids[0] + off, 4) for off in offsets]

    for n, block in enumerate(blocks):
        for e in range(LIST):
            place = table[(side * 4 + block) * LIST + e]
            to = slice((n * LIST + e) * BLK, (n * LIST + e + 1) * BLK)

            def from_array(ref, place=place, to=to):
                def go():
                    held[to, :] = ref[pl.ds(pl.multiple_of(lax.rem(place, 64) * BLK, BLK), BLK), :]

                return go

            lax.switch(lax.div(place, 64), [from_array(r) for r in arrays])

    rows = lax.broadcasted_iota(jnp.int32, (BLK, BLK), 0)
    lanes = lax.broadcasted_iota(jnp.int32, (BLK, BLK), 1)
    for n, block in enumerate(blocks):
        at = pl.ds(pl.multiple_of(block * BLK, BLK), BLK)
        position = rows + (ids[6 + side] + block * BLK)
        begin, end = jnp.zeros_like(rows), 0
        for d in range(lengths.shape[0]):
            end = end + lengths[d]
            begin = jnp.where(position >= end, end, begin)
        bias = []
        for e in range(LIST):
            index = lanes + table[(8 + side * 4 + block) * LIST + e]
            bias.append(jnp.where((index <= position) & (index >= begin), 0.0, NEG_LARGE))
        bias = jnp.concatenate(bias, axis=1)
        span = slice(n * LIST * BLK, (n + 1) * LIST * BLK)
        keys = held[span, :HD]
        values = held[span, HD:]
        part = jnp.concatenate([query[at, h * HD : (h + 1) * HD] for h in range(4)])
        scores = lax.dot_general(part, keys, (((1,), (1,)), ((), ())), preferred_element_type=F32)
        rounded, totals = [], []
        for h in range(4):
            masked = scores[h * BLK : (h + 1) * BLK] + bias
            weights = jnp.exp(masked - jnp.max(masked, axis=1, keepdims=True))
            totals.append(jnp.sum(weights, axis=1, keepdims=True))
            rounded.append(weights.astype(BF16))
        mixed = jnp.dot(jnp.concatenate(rounded), values, preferred_element_type=F32)
        for h in range(4):
            done = mixed[h * BLK : (h + 1) * BLK] / totals[h]
            out[n * BLK : (n + 1) * BLK, h * HD : (h + 1) * HD] = done.astype(BF16)


def attend(side, offsets, ids, table, lengths, query, arrays):
    count = len(offsets)
    smem = pl.BlockSpec(memory_space=pltpu.SMEM)
    vmem = pl.BlockSpec(memory_space=pltpu.VMEM)
    work = count * 4 * BLK * LIST * BLK
    return pl.pallas_call(
        functools.partial(attend_kernel, side, offsets, len(arrays)),
        in_specs=[smem] * 3 + [vmem] * (1 + len(arrays)),
        out_specs=vmem,
        out_shape=jax.ShapeDtypeStruct((count * BLK, 4 * HD), BF16),
        scratch_shapes=[pltpu.VMEM((count * LIST * BLK, 2 * HD), BF16)],
        compiler_params=pltpu.CompilerParams(vmem_limit_bytes=VMEM),
        cost_estimate=pl.CostEstimate(
            flops=4 * work * HD, bytes_accessed=count << 20, transcendentals=work
        ),
    )(ids, table, lengths, query, *arrays)


def heads_in_order(core, mine, other):
    return jnp.concatenate(
        [jnp.where(core == 0, mine, other), jnp.where(core == 0, other, mine)], axis=1
    )


def far_kernel(core, mine, other, w_left, w_right, left, right):
    rows = heads_in_order(core[0], mine[...], other[...])
    left[...] = jnp.dot(rows, w_left[...], preferred_element_type=F32).astype(BF16)
    right[...] = jnp.dot(rows, w_right[...], preferred_element_type=F32).astype(BF16)


TILE = 512


def project_far(core, mine, other, wo):
    rows, cols = mine.shape[0], wo.shape[1]
    n = cols // TILE // 2
    whole = pl.BlockSpec(mine.shape, lambda j, core: (0, 0))
    out = jax.ShapeDtypeStruct((rows, cols // 2), BF16)
    return pl.pallas_call(
        far_kernel,
        grid_spec=pltpu.PrefetchScalarGridSpec(
            num_scalar_prefetch=1,
            grid=(n,),
            in_specs=[
                whole,
                whole,
                pl.BlockSpec((wo.shape[0], TILE), lambda j, core: (0, j)),
                pl.BlockSpec((wo.shape[0], TILE), lambda j, core: (0, j + n)),
            ],
            out_specs=[pl.BlockSpec((rows, TILE), lambda j, core: (0, j))] * 2,
        ),
        out_shape=[out, out],
        compiler_params=pltpu.CompilerParams(vmem_limit_bytes=VMEM),
        cost_estimate=pl.CostEstimate(
            flops=2 * rows * wo.shape[0] * cols, bytes_accessed=10 << 20, transcendentals=0
        ),
    )(core, mine, other, wo, wo)


def near_kernel(n, core, mine, other, w, left, right, to_after, to_before):
    j = pl.program_id(0)
    rows = heads_in_order(core[0], mine[...], other[...])
    part = jnp.dot(rows, w[...], preferred_element_type=F32)

    @pl.when(j < n)
    def _():
        to_after[...] = (part[:BLK] + left[...].astype(F32)).astype(BF16)
        to_before[...] = part[BLK:].astype(BF16)

    @pl.when(j >= n)
    def _():
        to_after[...] = part[:BLK].astype(BF16)
        to_before[...] = (part[BLK:] + right[...].astype(F32)).astype(BF16)


def project_near(core, mine, other, wo, left, right):
    cols = wo.shape[1]
    n = cols // TILE // 2
    whole = pl.BlockSpec(mine.shape, lambda j, core: (0, 0))
    out = jax.ShapeDtypeStruct((BLK, cols), BF16)
    return pl.pallas_call(
        functools.partial(near_kernel, n),
        grid_spec=pltpu.PrefetchScalarGridSpec(
            num_scalar_prefetch=1,
            grid=(2 * n,),
            in_specs=[
                whole,
                whole,
                pl.BlockSpec((wo.shape[0], TILE), lambda j, core: (0, j)),
                pl.BlockSpec((BLK, TILE), lambda j, core: (0, jnp.minimum(j, n - 1))),
                pl.BlockSpec((BLK, TILE), lambda j, core: (0, jnp.maximum(j - n, 0))),
            ],
            out_specs=[pl.BlockSpec((BLK, TILE), lambda j, core: (0, j))] * 2,
        ),
        out_shape=[out, out],
        compiler_params=pltpu.CompilerParams(vmem_limit_bytes=VMEM),
        cost_estimate=pl.CostEstimate(
            flops=4 * BLK * wo.shape[0] * cols, bytes_accessed=11 << 20, transcendentals=0
        ),
    )(core, mine, other, wo, left, right)


def own_kernel(core, mine, other, w, out):
    rows = heads_in_order(core[0], mine[...], other[...])
    out[...] = jnp.dot(rows, w[...], preferred_element_type=F32)


def project_own(core, mine, other, wo):
    cols = wo.shape[1]
    whole = pl.BlockSpec(mine.shape, lambda j, core: (0, 0))
    return pl.pallas_call(
        own_kernel,
        grid_spec=pltpu.PrefetchScalarGridSpec(
            num_scalar_prefetch=1,
            grid=(cols // TILE,),
            in_specs=[whole, whole, pl.BlockSpec((wo.shape[0], TILE), lambda j, core: (0, j))],
            out_specs=pl.BlockSpec((BLK, TILE), lambda j, core: (0, j)),
        ),
        out_shape=jax.ShapeDtypeStruct((BLK, cols), F32),
        compiler_params=pltpu.CompilerParams(vmem_limit_bytes=VMEM),
        cost_estimate=pl.CostEstimate(
            flops=2 * BLK * wo.shape[0] * cols, bytes_accessed=10 << 20, transcendentals=0
        ),
    )(core, mine, other, wo)


def rope_tables(positions):
    frequency = ROPE_BASE ** (-(jnp.arange(HD // 2, dtype=F32) * 2.0 / HD))
    angles = positions.astype(F32)[:, None] * frequency[None, :]
    cosine, sine = jnp.cos(angles), jnp.sin(angles)
    return jnp.concatenate([cosine, cosine], axis=1), jnp.concatenate([-sine, sine], axis=1)


def fresh_entries(pattern):
    equal = pattern[:, :, None] == pattern[:, None, :]
    earlier = jnp.tril(jnp.ones((LIST, LIST), dtype=bool), -1)
    return jnp.logical_not(jnp.any(equal & earlier[None], axis=2))


def block_places(pattern, me):
    core, y, z = me % 2, (me // 2) % 4, me // 8
    per = 4 // CHUNKS
    chip = pattern // 8
    from_z, from_y = chip // 4, chip % 4
    other, local = ((pattern // 4) % 2 != core).astype(jnp.int32), pattern % 4
    along_one = jnp.where(core == 0, z - from_z, y - from_y) % 4
    along_two = jnp.where(core == 0, y - from_y, z - from_z) % 4
    slots = [jnp.where(u == 3, 2, jnp.where(u == 2, 3, u)) for u in (along_one, along_two)]
    array = (local // per) * 4 + slots[1]
    return array * 64 + (slots[0] * 2 + other) * per + local % per


def after(u, *others):
    return lax.optimization_barrier((u, *others))[0]


def on_device(x_tokens, w_query, w_key, w_value, w_output, pattern, doc_lengths):
    rows = x_tokens.shape[0]
    tp, me = lax.axis_index("tp"), lax.axis_index("ctx")
    core = me % 2
    length = rows // CHUNKS
    ids = jnp.stack(
        [tp, (tp + 3) % 4, (tp + 1) % 4, (tp + 2) % 4, core, 1 - core, me * rows, (me ^ 1) * rows]
    ).astype(jnp.int32)
    cos, sin = rope_tables(me * rows + jnp.arange(rows, dtype=jnp.int32))
    listed = jnp.concatenate([pattern, core_swap(pattern)])
    base = jnp.where(fresh_entries(listed), listed * BLK, 1 << 24)
    table = jnp.concatenate([block_places(listed, me), base]).astype(jnp.int32).reshape(-1)

    first, second = x_tokens[:length], x_tokens[length:]
    first_before, first_after = send_tp(first, 1), send_tp(first, -1)
    first_far = send_tp(after(first_before, ids, cos, sin, table), 1)
    second_after = send_tp(after(second, first_after), -1)
    second_before = send_tp(after(second, first_far), 1)
    second_far = send_tp(second_after, -1)
    sources = [
        (first, first_before, first_after, first_far),
        (second, second_before, second_after, second_far),
    ]

    gathered, query = [], []
    for chunk in range(CHUNKS):
        part = slice(chunk * length, (chunk + 1) * length)
        mine, theirs = project_kv(ids, sources[chunk], w_key, w_value, cos[part], sin[part])
        shard = pack(mine, core_swap(theirs))
        line = pack(shard, *[send_one(shard, step) for step in (1, -1, 2)])
        near = {step: send_two(line, step) for step in (1, -1)}
        made = project_q(ids, 1 - chunk, sources, w_query, cos, sin)
        query.append(made if chunk else core_swap(made))
        way = 1 - 2 * chunk
        gathered += [line, near[1], near[-1], send_two(after(near[way], made), way)]

    def attended(*offsets):
        other = core_swap(attend(1, offsets, ids, table, doc_lengths, query[0], gathered))
        return attend(0, offsets, ids, table, doc_lengths, query[1], gathered), other

    core_id = ids[4:5]
    left, right = project_far(core_id, *attended(2), w_output)
    left, right = send_tp(left, 1), send_tp(right, -1)
    to_after, to_before = project_near(core_id, *attended(1, 3), w_output, left, right)
    from_before, from_after = send_tp(to_after, 1), send_tp(to_before, -1)
    own = project_own(core_id, *attended(0), w_output)
    return (own + from_before.astype(F32) + from_after.astype(F32)).astype(BF16)


def solution(mesh):
    return jax.shard_map(
        on_device,
        mesh=mesh,
        in_specs=(
            P("ctx", "tp"),
            P(None, "tp"),
            P(None, "tp"),
            P(None, "tp"),
            P("tp", None),
            P("ctx", None),
            P(),
        ),
        out_specs=P(("ctx", "tp"), None),
        check_vma=False,
    )
```

```python
import functools

import jax
import jax.numpy as jnp
from jax import lax
from jax.experimental import pallas as pl
from jax.experimental.pallas import tpu as pltpu
from jax.sharding import PartitionSpec as P

HD = 128
BLK = 128
LIST = 8
ROPE_BASE = 500000.0
NEG_LARGE = -1e30
CHUNKS = 2
VMEM = 20 << 20
BF16 = jnp.bfloat16
F32 = jnp.float32


def ctx_index(z, y, c):
    return ((z % 4) * 4 + (y % 4)) * 2 + c


def plane_pairs(step, first):
    pairs = []
    for z in range(4):
        for y in range(4):
            for c in range(2):
                along_z = (c == 0) == first
                to = ctx_index(z + step, y, c) if along_z else ctx_index(z, y + step, c)
                pairs.append((ctx_index(z, y, c), to))
    return pairs


CORE_PAIRS = [(i, i ^ 1) for i in range(32)]


def tp_pairs(step):
    return [
        (i * 4 + t, i * 4 + (t + (step if i % 2 == 0 else -step)) % 4) for i in range(32) for t in range(4)
    ]


def cost(us):
    return pl.CostEstimate(flops=int(us * 1.1e9), bytes_accessed=0, transcendentals=0)


def core_swap(u):
    return lax.ppermute(u, "ctx", CORE_PAIRS)


def send_tp(u, step):
    return lax.ppermute(u, ("ctx", "tp"), tp_pairs(step))


def send_one(u, step):
    return lax.ppermute(u, "ctx", plane_pairs(step, True))


def send_two(u, step):
    return lax.ppermute(u, "ctx", plane_pairs(step, False))


def roped(u, cosine, sine):
    return u * cosine + pltpu.roll(u, HD // 2, 1) * sine


def kv_part_kernel(n, ids, *refs):
    sources, (wk, wv, tk, tv) = refs[:n], refs[n:]
    step = pl.program_id(0)
    for at, ref in enumerate(sources):

        @pl.when(step == at)
        def _(at=at, ref=ref):
            for w, total in ((wk, tk), (wv, tv)):
                part = jnp.dot(ref[...], w[...], preferred_element_type=F32)
                if at == 0:
                    total[...] = part
                else:
                    total[...] += part


def kv_part(ids, sources, wk, wv):
    n = len(sources)
    rows, depth = sources[0].shape
    whole = pl.BlockSpec((rows, depth), lambda k, ids: (0, 0))
    w_spec = pl.BlockSpec((depth, 2 * HD), lambda k, ids: (ids[k], 0))
    out = jax.ShapeDtypeStruct((rows, 2 * HD), F32)
    return pl.pallas_call(
        functools.partial(kv_part_kernel, n),
        grid_spec=pltpu.PrefetchScalarGridSpec(
            num_scalar_prefetch=1,
            grid=(n,),
            in_specs=[whole] * n + [w_spec, w_spec],
            out_specs=[pl.BlockSpec((rows, 2 * HD), lambda k, ids: (0, 0))] * 2,
        ),
        out_shape=[out, out],
        compiler_params=pltpu.CompilerParams(vmem_limit_bytes=VMEM),
        cost_estimate=cost(len(sources)),
    )(ids, *sources, wk, wv)


def kv_kernel(ids, far, wk, wv, pk, pv, cos, sin, mine, theirs):
    keys = pk[...] + jnp.dot(far[...], wk[...], preferred_element_type=F32)
    vals = pv[...] + jnp.dot(far[...], wv[...], preferred_element_type=F32)
    cosine, sine = cos[...], sin[...]
    keys = [roped(keys[:, h * HD : (h + 1) * HD], cosine, sine).astype(BF16) for h in range(2)]
    vals = [vals[:, h * HD : (h + 1) * HD].astype(BF16) for h in range(2)]

    for core in range(2):

        @pl.when(ids[4] == core)
        def _(core=core):
            mine[:, :HD] = keys[core]
            mine[:, HD:] = vals[core]
            theirs[:, :HD] = keys[1 - core]
            theirs[:, HD:] = vals[1 - core]


def project_kv(ids, chunk, far, parts, wk, wv, cos, sin):
    rows, depth = far.shape
    whole = lambda shape: pl.BlockSpec(shape, lambda k, ids: (0, 0))
    w_spec = pl.BlockSpec((depth, 2 * HD), lambda k, ids: (ids[3], 0))
    table = pl.BlockSpec((rows, HD), lambda k, ids: (chunk, 0))
    out = jax.ShapeDtypeStruct((rows, 2 * HD), BF16)
    return pl.pallas_call(
        kv_kernel,
        grid_spec=pltpu.PrefetchScalarGridSpec(
            num_scalar_prefetch=1,
            grid=(1,),
            in_specs=[whole(far.shape), w_spec, w_spec, whole((rows, 2 * HD)), whole((rows, 2 * HD)), table, table],
            out_specs=[whole((rows, 2 * HD))] * 2,
        ),
        out_shape=[out, out],
        compiler_params=pltpu.CompilerParams(vmem_limit_bytes=VMEM),
        cost_estimate=cost(1),
    )(ids, far, wk, wv, *parts, cos, sin)


def q_kernel(ids, *refs):
    parts, (wq, cos, sin, out) = [refs[4 * k : 4 * k + 4] for k in range(CHUNKS)], refs[4 * CHUNKS :]
    depth = parts[0][0].shape[1]
    at = [pl.ds(pl.multiple_of(ids[k] * depth, depth), depth) for k in range(4)]
    for chunk, sources in enumerate(parts):
        rows = sources[0].shape[0]
        span = slice(chunk * rows, (chunk + 1) * rows)
        total = sum(jnp.dot(sources[k][...], wq[at[k], :], preferred_element_type=F32) for k in range(4))
        cosine, sine = cos[span, :], sin[span, :]
        for h in range(2):
            turned = roped(total[:, h * HD : (h + 1) * HD], cosine, sine) * HD ** (-0.5)
            out[span, h * HD : (h + 1) * HD] = turned.astype(BF16)


def project_q(ids, side, sources, wq, cos, sin):
    rows, inner = cos.shape[0], wq.shape[0]
    flat = [u for part in sources for u in part]
    whole = lambda u: pl.BlockSpec(u.shape, lambda j, ids: (0, 0))
    return pl.pallas_call(
        q_kernel,
        grid_spec=pltpu.PrefetchScalarGridSpec(
            num_scalar_prefetch=1,
            grid=(2,),
            in_specs=[whole(u) for u in flat]
            + [
                pl.BlockSpec((inner, 2 * HD), lambda j, ids: (0, 2 * ids[4 + side] + j)),
                whole(cos),
                whole(sin),
            ],
            out_specs=pl.BlockSpec((rows, 2 * HD), lambda j, ids: (0, j)),
        ),
        out_shape=jax.ShapeDtypeStruct((rows, 4 * HD), BF16),
        compiler_params=pltpu.CompilerParams(vmem_limit_bytes=VMEM),
        cost_estimate=cost(5),
    )(ids, *flat, wq, cos, sin)


def pack_kernel(*refs):
    parts, out = refs[:-1], refs[-1]
    rows = parts[0].shape[0]
    for k, u in enumerate(parts):
        out[k * rows : (k + 1) * rows, :] = u[...]


def pack(*parts):
    rows, cols = parts[0].shape
    vmem = pl.BlockSpec(memory_space=pltpu.VMEM)
    return pl.pallas_call(
        pack_kernel,
        in_specs=[vmem] * len(parts),
        out_specs=vmem,
        out_shape=jax.ShapeDtypeStruct((len(parts) * rows, cols), parts[0].dtype),
        compiler_params=pltpu.CompilerParams(vmem_limit_bytes=VMEM),
        cost_estimate=cost(0.4),
    )(*parts)


def attend_kernel(side, steps, n_arrays, ids, table, lengths, query, *rest):
    arrays, (out, held) = rest[:n_arrays], rest[n_arrays:]
    turned = 1 - 2 * ids[4 + side]
    blocks = [lax.rem(ids[0] + 4 + step * turned, 4) for step in steps]

    for n, block in enumerate(blocks):
        for e in range(LIST):
            place = table[(side * 4 + block) * LIST + e]
            to = slice((n * LIST + e) * BLK, (n * LIST + e + 1) * BLK)

            def from_array(ref, place=place, to=to):
                def go():
                    held[to, :] = ref[pl.ds(pl.multiple_of(lax.rem(place, 64) * BLK, BLK), BLK), :]

                return go

            lax.switch(lax.div(place, 64), [from_array(r) for r in arrays])

    rows = lax.broadcasted_iota(jnp.int32, (BLK, BLK), 0)
    lanes = lax.broadcasted_iota(jnp.int32, (BLK, BLK), 1)
    for n, block in enumerate(blocks):
        at = pl.ds(pl.multiple_of(block * BLK, BLK), BLK)
        position = rows + (ids[6 + side] + block * BLK)
        begin, end = jnp.zeros_like(rows), 0
        for d in range(lengths.shape[0]):
            end = end + lengths[d]
            begin = jnp.where(position >= end, end, begin)
        bias = []
        for e in range(LIST):
            index = lanes + table[(8 + side * 4 + block) * LIST + e]
            bias.append(jnp.where((index <= position) & (index >= begin), 0.0, NEG_LARGE))
        bias = jnp.concatenate(bias, axis=1)
        span = slice(n * LIST * BLK, (n + 1) * LIST * BLK)
        keys = held[span, :HD]
        values = held[span, HD:]
        part = jnp.concatenate([query[at, h * HD : (h + 1) * HD] for h in range(4)])
        scores = lax.dot_general(part, keys, (((1,), (1,)), ((), ())), preferred_element_type=F32)
        rounded, totals = [], []
        for h in range(4):
            masked = scores[h * BLK : (h + 1) * BLK] + bias
            weights = jnp.exp(masked - jnp.max(masked, axis=1, keepdims=True))
            totals.append(jnp.sum(weights, axis=1, keepdims=True))
            rounded.append(weights.astype(BF16))
        mixed = jnp.dot(jnp.concatenate(rounded), values, preferred_element_type=F32)
        for h in range(4):
            done = mixed[h * BLK : (h + 1) * BLK] / totals[h]
            out[n * BLK : (n + 1) * BLK, h * HD : (h + 1) * HD] = done.astype(BF16)


def attend(side, steps, ids, table, lengths, query, arrays):
    count = len(steps)
    smem = pl.BlockSpec(memory_space=pltpu.SMEM)
    vmem = pl.BlockSpec(memory_space=pltpu.VMEM)
    return pl.pallas_call(
        functools.partial(attend_kernel, side, steps, len(arrays)),
        in_specs=[smem] * 3 + [vmem] * (1 + len(arrays)),
        out_specs=vmem,
        out_shape=jax.ShapeDtypeStruct((count * BLK, 4 * HD), BF16),
        scratch_shapes=[pltpu.VMEM((count * LIST * BLK, 2 * HD), BF16)],
        compiler_params=pltpu.CompilerParams(vmem_limit_bytes=VMEM),
        cost_estimate=cost(1 + 1.2 * count),
    )(ids, table, lengths, query, *arrays)


def heads_in_order(core, mine, other):
    return jnp.concatenate(
        [jnp.where(core == 0, mine, other), jnp.where(core == 0, other, mine)], axis=1
    )


TILE = 512


def out_kernel(core, mine, other, w, *outs):
    rows = heads_in_order(core[0], mine[...], other[...])
    part = jnp.dot(rows, w[...], preferred_element_type=F32)
    for k, out in enumerate(outs):
        out[...] = part[k * BLK : (k + 1) * BLK].astype(out.dtype)


def project_out(core, mine, other, wo, types):
    cols = wo.shape[1]
    whole = pl.BlockSpec(mine.shape, lambda j, core: (0, 0))
    return pl.pallas_call(
        out_kernel,
        grid_spec=pltpu.PrefetchScalarGridSpec(
            num_scalar_prefetch=1,
            grid=(cols // TILE,),
            in_specs=[whole, whole, pl.BlockSpec((wo.shape[0], TILE), lambda j, core: (0, j))],
            out_specs=[pl.BlockSpec((BLK, TILE), lambda j, core: (0, j))] * len(types),
        ),
        out_shape=[jax.ShapeDtypeStruct((BLK, cols), t) for t in types],
        compiler_params=pltpu.CompilerParams(vmem_limit_bytes=VMEM),
        cost_estimate=cost(2 + len(types)),
    )(core, mine, other, wo)


def rope_tables(positions):
    frequency = ROPE_BASE ** (-(jnp.arange(HD // 2, dtype=F32) * 2.0 / HD))
    angles = positions.astype(F32)[:, None] * frequency[None, :]
    cosine, sine = jnp.cos(angles), jnp.sin(angles)
    return jnp.concatenate([cosine, cosine], axis=1), jnp.concatenate([-sine, sine], axis=1)


def fresh_entries(pattern):
    equal = pattern[:, :, None] == pattern[:, None, :]
    earlier = jnp.tril(jnp.ones((LIST, LIST), dtype=bool), -1)
    return jnp.logical_not(jnp.any(equal & earlier[None], axis=2))


def block_places(pattern, me):
    core, y, z = me % 2, (me // 2) % 4, me // 8
    per = 4 // CHUNKS
    chip = pattern // 8
    from_z, from_y = chip // 4, chip % 4
    other, local = ((pattern // 4) % 2 != core).astype(jnp.int32), pattern % 4
    along_one = jnp.where(core == 0, z - from_z, y - from_y) % 4
    along_two = jnp.where(core == 0, y - from_y, z - from_z) % 4
    slots = [jnp.where(u == 3, 2, jnp.where(u == 2, 3, u)) for u in (along_one, along_two)]
    array = (local // per) * 4 + slots[1]
    return array * 64 + (slots[0] * 2 + other) * per + local % per


def after(u, *others):
    return lax.optimization_barrier((u, *others))[0]


def on_device(x_tokens, w_query, w_key, w_value, w_output, pattern, doc_lengths):
    rows = x_tokens.shape[0]
    tp, me = lax.axis_index("tp"), lax.axis_index("ctx")
    core = me % 2
    length = rows // CHUNKS
    ids = jnp.stack(
        [tp, (tp + 3 + 2 * core) % 4, (tp + 1 + 2 * core) % 4, (tp + 2) % 4, core, 1 - core, me * rows, (me ^ 1) * rows]
    ).astype(jnp.int32)
    cos, sin = rope_tables(me * rows + jnp.arange(rows, dtype=jnp.int32))
    listed = jnp.concatenate([pattern, core_swap(pattern)])
    base = jnp.where(fresh_entries(listed), listed * BLK, 1 << 24)
    table = jnp.concatenate([block_places(listed, me), base]).astype(jnp.int32).reshape(-1)

    first, second = x_tokens[:length], x_tokens[length:]
    first_before, first_after = send_tp(first, 1), send_tp(first, -1)
    first_far = send_tp(after(first_before, ids, cos, sin, table), 1)
    second_before = send_tp(after(second, first_before, first_after), 1)
    second_after = send_tp(after(second, first_before, first_after), -1)
    parts = kv_part(ids, (first, first_before, first_after), w_key, w_value)
    mine, theirs = project_kv(ids, 0, first_far, parts, w_key, w_value, cos, sin)
    second_far = send_tp(after(second_before, theirs), 1)
    sources = [
        (first, first_before, first_after, first_far),
        (second, second_before, second_after, second_far),
    ]
    gathered = []
    for chunk in range(CHUNKS):
        if chunk:
            held = after(second, line)
            parts = kv_part(ids, (held, second_before, second_after), w_key, w_value)
            mine, theirs = project_kv(ids, 1, second_far, parts, w_key, w_value, cos, sin)
        shard = pack(mine, core_swap(theirs))
        line = pack(shard, *[send_one(shard, step) for step in (1, -1, 2)])
        near = {step: send_two(line, step) for step in (1, -1)}
        way = 1 - 2 * chunk
        onward = near[way]
        if chunk:
            query = [project_q(ids, side, sources, w_query, cos, sin) for side in (0, 1)]
            onward = after(onward, *query)
        gathered += [line, near[1], near[-1], send_two(onward, way)]
    query[1] = core_swap(query[1])

    def attended(*steps):
        other = core_swap(attend(1, steps, ids, table, doc_lengths, query[1], gathered))
        return attend(0, steps, ids, table, doc_lengths, query[0], gathered), other

    core_id = ids[4:5]
    (far,) = project_out(core_id, *attended(2), w_output, (BF16,))
    arrived = send_tp(far, 1)
    ahead, behind = project_out(core_id, *attended(1, -1), w_output, (F32, BF16))
    from_after = send_tp(behind, -1)
    from_before = send_tp((ahead + arrived.astype(F32)).astype(BF16), 1)
    (own,) = project_out(core_id, *attended(0), w_output, (F32,))
    return (own + from_before.astype(F32) + from_after.astype(F32)).astype(BF16)


def solution(mesh):
    return jax.shard_map(
        on_device,
        mesh=mesh,
        in_specs=(
            P("ctx", "tp"),
            P(None, "tp"),
            P(None, "tp"),
            P(None, "tp"),
            P("tp", None),
            P("ctx", None),
            P(),
        ),
        out_specs=P(("ctx", "tp"), None),
        check_vma=False,
    )
```

```python
import functools

import jax
import jax.numpy as jnp
from jax import lax
from jax.experimental import pallas as pl
from jax.experimental.pallas import tpu as pltpu
from jax.sharding import PartitionSpec as P

HD = 128
BLK = 128
LIST = 8
ROPE_BASE = 500000.0
NEG_LARGE = -1e30
CHUNKS = 2
VMEM = 20 << 20
BF16 = jnp.bfloat16
F32 = jnp.float32


def ctx_index(z, y, c):
    return ((z % 4) * 4 + (y % 4)) * 2 + c


def plane_pairs(step, first):
    pairs = []
    for z in range(4):
        for y in range(4):
            for c in range(2):
                along_z = (c == 0) == first
                to = ctx_index(z + step, y, c) if along_z else ctx_index(z, y + step, c)
                pairs.append((ctx_index(z, y, c), to))
    return pairs


CORE_PAIRS = [(i, i ^ 1) for i in range(32)]


def tp_pairs(step):
    return [
        (i * 4 + t, i * 4 + (t + (step if i % 2 == 0 else -step)) % 4) for i in range(32) for t in range(4)
    ]


def cost(us):
    return pl.CostEstimate(flops=int(us * 1.1e9), bytes_accessed=0, transcendentals=0)


def core_swap(u):
    return lax.ppermute(u, "ctx", CORE_PAIRS)


def send_tp(u, step):
    return lax.ppermute(u, ("ctx", "tp"), tp_pairs(step))


def send_one(u, step):
    return lax.ppermute(u, "ctx", plane_pairs(step, True))


def send_two(u, step):
    return lax.ppermute(u, "ctx", plane_pairs(step, False))


def roped(u, cosine, sine):
    return u * cosine + pltpu.roll(u, HD // 2, 1) * sine


def kv_part_kernel(n, ids, *refs):
    sources, (wk, wv, tk, tv) = refs[:n], refs[n:]
    step = pl.program_id(0)
    for at, ref in enumerate(sources):

        @pl.when(step == at)
        def _(at=at, ref=ref):
            for w, total in ((wk, tk), (wv, tv)):
                part = jnp.dot(ref[...], w[...], preferred_element_type=F32)
                if at == 0:
                    total[...] = part
                else:
                    total[...] += part


def kv_part(ids, sources, wk, wv):
    n = len(sources)
    rows, depth = sources[0].shape
    whole = pl.BlockSpec((rows, depth), lambda k, ids: (0, 0))
    w_spec = pl.BlockSpec((depth, 2 * HD), lambda k, ids: (ids[k], 0))
    out = jax.ShapeDtypeStruct((rows, 2 * HD), F32)
    return pl.pallas_call(
        functools.partial(kv_part_kernel, n),
        grid_spec=pltpu.PrefetchScalarGridSpec(
            num_scalar_prefetch=1,
            grid=(n,),
            in_specs=[whole] * n + [w_spec, w_spec],
            out_specs=[pl.BlockSpec((rows, 2 * HD), lambda k, ids: (0, 0))] * 2,
        ),
        out_shape=[out, out],
        compiler_params=pltpu.CompilerParams(vmem_limit_bytes=VMEM),
        cost_estimate=cost(len(sources)),
    )(ids, *sources, wk, wv)


def kv_kernel(ids, far, wk, wv, pk, pv, cos, sin, mine, theirs):
    keys = pk[...] + jnp.dot(far[...], wk[...], preferred_element_type=F32)
    vals = pv[...] + jnp.dot(far[...], wv[...], preferred_element_type=F32)
    cosine, sine = cos[...], sin[...]
    keys = [roped(keys[:, h * HD : (h + 1) * HD], cosine, sine).astype(BF16) for h in range(2)]
    vals = [vals[:, h * HD : (h + 1) * HD].astype(BF16) for h in range(2)]

    for core in range(2):

        @pl.when(ids[4] == core)
        def _(core=core):
            mine[:, :HD] = keys[core]
            mine[:, HD:] = vals[core]
            theirs[:, :HD] = keys[1 - core]
            theirs[:, HD:] = vals[1 - core]


def project_kv(ids, chunk, far, parts, wk, wv, cos, sin):
    rows, depth = far.shape
    whole = lambda shape: pl.BlockSpec(shape, lambda k, ids: (0, 0))
    w_spec = pl.BlockSpec((depth, 2 * HD), lambda k, ids: (ids[3], 0))
    table = pl.BlockSpec((rows, HD), lambda k, ids: (chunk, 0))
    out = jax.ShapeDtypeStruct((rows, 2 * HD), BF16)
    return pl.pallas_call(
        kv_kernel,
        grid_spec=pltpu.PrefetchScalarGridSpec(
            num_scalar_prefetch=1,
            grid=(1,),
            in_specs=[whole(far.shape), w_spec, w_spec, whole((rows, 2 * HD)), whole((rows, 2 * HD)), table, table],
            out_specs=[whole((rows, 2 * HD))] * 2,
        ),
        out_shape=[out, out],
        compiler_params=pltpu.CompilerParams(vmem_limit_bytes=VMEM),
        cost_estimate=cost(1),
    )(ids, far, wk, wv, *parts, cos, sin)


def q_kernel(ids, *refs):
    parts, (wq, cos, sin, out) = [refs[4 * k : 4 * k + 4] for k in range(CHUNKS)], refs[4 * CHUNKS :]
    depth = parts[0][0].shape[1]
    at = [pl.ds(pl.multiple_of(ids[k] * depth, depth), depth) for k in range(4)]
    for chunk, sources in enumerate(parts):
        rows = sources[0].shape[0]
        span = slice(chunk * rows, (chunk + 1) * rows)
        total = sum(jnp.dot(sources[k][...], wq[at[k], :], preferred_element_type=F32) for k in range(4))
        cosine, sine = cos[span, :], sin[span, :]
        for h in range(2):
            turned = roped(total[:, h * HD : (h + 1) * HD], cosine, sine) * HD ** (-0.5)
            out[span, h * HD : (h + 1) * HD] = turned.astype(BF16)


def project_q(ids, side, sources, wq, cos, sin):
    rows, inner = cos.shape[0], wq.shape[0]
    flat = [u for part in sources for u in part]
    whole = lambda u: pl.BlockSpec(u.shape, lambda j, ids: (0, 0))
    return pl.pallas_call(
        q_kernel,
        grid_spec=pltpu.PrefetchScalarGridSpec(
            num_scalar_prefetch=1,
            grid=(2,),
            in_specs=[whole(u) for u in flat]
            + [
                pl.BlockSpec((inner, 2 * HD), lambda j, ids: (0, 2 * ids[4 + side] + j)),
                whole(cos),
                whole(sin),
            ],
            out_specs=pl.BlockSpec((rows, 2 * HD), lambda j, ids: (0, j)),
        ),
        out_shape=jax.ShapeDtypeStruct((rows, 4 * HD), BF16),
        compiler_params=pltpu.CompilerParams(vmem_limit_bytes=VMEM),
        cost_estimate=cost(5),
    )(ids, *flat, wq, cos, sin)


def pack_kernel(*refs):
    parts, out = refs[:-1], refs[-1]
    rows = parts[0].shape[0]
    for k, u in enumerate(parts):
        out[k * rows : (k + 1) * rows, :] = u[...]


def pack(*parts):
    rows, cols = parts[0].shape
    vmem = pl.BlockSpec(memory_space=pltpu.VMEM)
    return pl.pallas_call(
        pack_kernel,
        in_specs=[vmem] * len(parts),
        out_specs=vmem,
        out_shape=jax.ShapeDtypeStruct((len(parts) * rows, cols), parts[0].dtype),
        compiler_params=pltpu.CompilerParams(vmem_limit_bytes=VMEM),
        cost_estimate=cost(0.4),
    )(*parts)


def attend_kernel(side, steps, n_arrays, ids, table, lengths, query, *rest):
    arrays, (out, held) = rest[:n_arrays], rest[n_arrays:]
    turned = 1 - 2 * ids[4 + side]
    blocks = [lax.rem(ids[0] + 4 + step * turned, 4) for step in steps]

    for n, block in enumerate(blocks):
        for e in range(LIST):
            place = table[(side * 4 + block) * LIST + e]
            to = slice((n * LIST + e) * BLK, (n * LIST + e + 1) * BLK)

            def from_array(ref, place=place, to=to):
                def go():
                    held[to, :] = ref[pl.ds(pl.multiple_of(lax.rem(place, 64) * BLK, BLK), BLK), :]

                return go

            lax.switch(lax.div(place, 64), [from_array(r) for r in arrays])

    rows = lax.broadcasted_iota(jnp.int32, (BLK, BLK), 0)
    lanes = lax.broadcasted_iota(jnp.int32, (BLK, BLK), 1)
    for n, block in enumerate(blocks):
        at = pl.ds(pl.multiple_of(block * BLK, BLK), BLK)
        position = rows + (ids[6 + side] + block * BLK)
        begin, end = jnp.zeros_like(rows), 0
        for d in range(lengths.shape[0]):
            end = end + lengths[d]
            begin = jnp.where(position >= end, end, begin)
        bias = []
        for e in range(LIST):
            index = lanes + table[(8 + side * 4 + block) * LIST + e]
            bias.append(jnp.where((index <= position) & (index >= begin), 0.0, NEG_LARGE))
        bias = jnp.concatenate(bias, axis=1)
        span = slice(n * LIST * BLK, (n + 1) * LIST * BLK)
        keys = held[span, :HD]
        values = held[span, HD:]
        part = jnp.concatenate([query[at, h * HD : (h + 1) * HD] for h in range(4)])
        scores = lax.dot_general(part, keys, (((1,), (1,)), ((), ())), preferred_element_type=F32)
        rounded, totals = [], []
        for h in range(4):
            masked = scores[h * BLK : (h + 1) * BLK] + bias
            weights = jnp.exp(masked - jnp.max(masked, axis=1, keepdims=True))
            totals.append(jnp.sum(weights, axis=1, keepdims=True))
            rounded.append(weights.astype(BF16))
        mixed = jnp.dot(jnp.concatenate(rounded), values, preferred_element_type=F32)
        for h in range(4):
            done = mixed[h * BLK : (h + 1) * BLK] / totals[h]
            out[n * BLK : (n + 1) * BLK, h * HD : (h + 1) * HD] = done.astype(BF16)


def attend(side, steps, ids, table, lengths, query, arrays):
    count = len(steps)
    smem = pl.BlockSpec(memory_space=pltpu.SMEM)
    vmem = pl.BlockSpec(memory_space=pltpu.VMEM)
    return pl.pallas_call(
        functools.partial(attend_kernel, side, steps, len(arrays)),
        in_specs=[smem] * 3 + [vmem] * (1 + len(arrays)),
        out_specs=vmem,
        out_shape=jax.ShapeDtypeStruct((count * BLK, 4 * HD), BF16),
        scratch_shapes=[pltpu.VMEM((count * LIST * BLK, 2 * HD), BF16)],
        compiler_params=pltpu.CompilerParams(vmem_limit_bytes=VMEM),
        cost_estimate=cost(1 + 1.2 * count),
    )(ids, table, lengths, query, *arrays)


def heads_in_order(core, mine, other):
    return jnp.concatenate(
        [jnp.where(core == 0, mine, other), jnp.where(core == 0, other, mine)], axis=1
    )


TILE = 512


def out_kernel(core, mine, other, w, *outs):
    rows = heads_in_order(core[0], mine[...], other[...])
    part = jnp.dot(rows, w[...], preferred_element_type=F32)
    for k, out in enumerate(outs):
        out[...] = part[k * BLK : (k + 1) * BLK].astype(out.dtype)


def project_out(core, mine, other, wo, types):
    cols = wo.shape[1]
    whole = pl.BlockSpec(mine.shape, lambda j, core: (0, 0))
    return pl.pallas_call(
        out_kernel,
        grid_spec=pltpu.PrefetchScalarGridSpec(
            num_scalar_prefetch=1,
            grid=(cols // TILE,),
            in_specs=[whole, whole, pl.BlockSpec((wo.shape[0], TILE), lambda j, core: (0, j))],
            out_specs=[pl.BlockSpec((BLK, TILE), lambda j, core: (0, j))] * len(types),
        ),
        out_shape=[jax.ShapeDtypeStruct((BLK, cols), t) for t in types],
        compiler_params=pltpu.CompilerParams(vmem_limit_bytes=VMEM),
        cost_estimate=cost(2 + len(types)),
    )(core, mine, other, wo)


def rope_tables(positions):
    frequency = ROPE_BASE ** (-(jnp.arange(HD // 2, dtype=F32) * 2.0 / HD))
    angles = positions.astype(F32)[:, None] * frequency[None, :]
    cosine, sine = jnp.cos(angles), jnp.sin(angles)
    return jnp.concatenate([cosine, cosine], axis=1), jnp.concatenate([-sine, sine], axis=1)


def fresh_entries(pattern):
    equal = pattern[:, :, None] == pattern[:, None, :]
    earlier = jnp.tril(jnp.ones((LIST, LIST), dtype=bool), -1)
    return jnp.logical_not(jnp.any(equal & earlier[None], axis=2))


def block_places(pattern, me):
    core, y, z = me % 2, (me // 2) % 4, me // 8
    per = 4 // CHUNKS
    chip = pattern // 8
    from_z, from_y = chip // 4, chip % 4
    other, local = ((pattern // 4) % 2 != core).astype(jnp.int32), pattern % 4
    along_one = jnp.where(core == 0, z - from_z, y - from_y) % 4
    along_two = jnp.where(core == 0, y - from_y, z - from_z) % 4
    slots = [jnp.where(u == 3, 2, jnp.where(u == 2, 3, u)) for u in (along_one, along_two)]
    array = (local // per) * 4 + slots[1]
    return array * 64 + (slots[0] * 2 + other) * per + local % per


def after(u, *others):
    return lax.optimization_barrier((u, *others))[0]


def on_device(x_tokens, w_query, w_key, w_value, w_output, pattern, doc_lengths):
    rows = x_tokens.shape[0]
    tp, me = lax.axis_index("tp"), lax.axis_index("ctx")
    core = me % 2
    length = rows // CHUNKS
    ids = jnp.stack(
        [tp, (tp + 3 + 2 * core) % 4, (tp + 1 + 2 * core) % 4, (tp + 2) % 4, core, 1 - core, me * rows, (me ^ 1) * rows]
    ).astype(jnp.int32)
    cos, sin = rope_tables(me * rows + jnp.arange(rows, dtype=jnp.int32))
    listed = jnp.concatenate([pattern, core_swap(pattern)])
    base = jnp.where(fresh_entries(listed), listed * BLK, 1 << 24)
    table = jnp.concatenate([block_places(listed, me), base]).astype(jnp.int32).reshape(-1)

    first, second = x_tokens[:length], x_tokens[length:]
    first_before, first_after = send_tp(first, 1), send_tp(first, -1)
    first_far = send_tp(after(first_before, ids, cos, sin, table), 1)
    second_before = send_tp(after(second, first_before, first_after), 1)
    second_after = send_tp(after(second, first_before, first_after), -1)
    parts = kv_part(ids, (first, first_before, first_after), w_key, w_value)
    mine, theirs = project_kv(ids, 0, first_far, parts, w_key, w_value, cos, sin)
    second_far = send_tp(after(second_before, theirs), 1)
    sources = [
        (first, first_before, first_after, first_far),
        (second, second_before, second_after, second_far),
    ]
    gathered = []
    for chunk in range(CHUNKS):
        if chunk:
            held = after(second, line)
            parts = kv_part(ids, (held, second_before, second_after), w_key, w_value)
            mine, theirs = project_kv(ids, 1, second_far, parts, w_key, w_value, cos, sin)
        shard = pack(mine, core_swap(theirs))
        line = pack(shard, *[send_one(shard, step) for step in (1, -1, 2)])
        near = {step: send_two(line, step) for step in (1, -1)}
        way = 1 - 2 * chunk
        onward = near[way]
        if chunk:
            query = [project_q(ids, side, sources, w_query, cos, sin) for side in (0, 1)]
            onward = after(onward, *query)
        gathered += [line, near[1], near[-1], send_two(onward, way)]
    query[1] = core_swap(query[1])

    def attended(step, *earlier):
        known = after(ids, *earlier)
        other = core_swap(attend(1, (step,), known, table, doc_lengths, query[1], gathered))
        return attend(0, (step,), known, table, doc_lengths, query[0], gathered), other

    core_id = ids[4:5]
    (far,) = project_out(core_id, *attended(2), w_output, (BF16,))
    arrived = send_tp(far, 1)
    (behind,) = project_out(core_id, *attended(-1, far), w_output, (BF16,))
    from_after = send_tp(behind, -1)
    (ahead,) = project_out(core_id, *attended(1, behind), w_output, (F32,))
    from_before = send_tp((ahead + arrived.astype(F32)).astype(BF16), 1)
    (own,) = project_out(core_id, *attended(0, ahead), w_output, (F32,))
    return (own + from_before.astype(F32) + from_after.astype(F32)).astype(BF16)


def solution(mesh):
    return jax.shard_map(
        on_device,
        mesh=mesh,
        in_specs=(
            P("ctx", "tp"),
            P(None, "tp"),
            P(None, "tp"),
            P(None, "tp"),
            P("tp", None),
            P("ctx", None),
            P(),
        ),
        out_specs=P(("ctx", "tp"), None),
        check_vma=False,
    )
```
